128 devices in a mesh: dp: 8 (over x, core), list: 16 (over y, z).
Axes of the slice: x: 4, y: 4, z: 4, core: 2. Of those that a mesh axis runs over, the one named last changes fastest.
Arguments:
- vectors: bfloat16 [32768, 768], P(('dp', 'list')), may hold values from -6 to 6
- centroids: bfloat16 [65536, 768], P('list'), may hold values from -6 to 6
- projection: bfloat16 [768, 128], replicated, may hold values from -0.21875 to 0.21875
- list_ids: int32 [32768, 2], replicated, may hold values from 0 to 65535, as said below
Outputs:
- placed: bfloat16 [131072, 128], P(('dp', 'list'))
- lowest_score: float32 [32768], P(('dp', 'list'))
The draws below stay inside these ranges and needn't reach their ends.
Inputs may be any that keep to these rules, and one draw needn't show every extreme that they name: `list_ids`: each row holds two different list ids. List j belongs to owner device (j % 8) * 16 + j // 4096. Device f holds rows f * 256 to f * 256 + 255; of the 512 ids of these rows at most 8 belong to any one owner device, and in every draw some owner device receives exactly 8 from every device's rows.
All inputs are finite; a program needn't handle non-finite values.
Results may differ from the reference program's by a relative error of at most 0.0039.
Values may be sent and summed in bfloat16 or wider, within the bound.
No kernel may reach another device: no remote copies, remote signals or barrier semaphores. Data moves between devices by JAX's collectives and lax.ppermute only.
A program may use at most 128 MiB of HBM per device.

```python
import jax
import jax.numpy as jnp
from jax import lax

D = 768
PREFIX = 256
PDIM = 128
LISTS = 65536
ROWS = 256
CAP = 8
VECTORS = 32768
N_DP = 8
N_LIST = 16


def draw_list_ids(key, part):
    key = jax.random.fold_in(key, 7)
    device_count = N_DP * N_LIST
    slot_count = device_count * CAP
    per_device = LISTS // N_LIST
    per_owner = per_device // N_DP
    base_key, block_key, list_key, order_key = jax.random.split(key, 4)
    hot_owner = jax.random.randint(jax.random.fold_in(base_key, 1), (), 0, device_count)
    owner_level = jax.random.randint(jax.random.fold_in(base_key, 2), (device_count,), 0, 4)
    owner_bias = owner_level * 4096 + jnp.where(jnp.arange(device_count) == hot_owner, 65536, 0)
    slot_owner = jnp.arange(slot_count) // CAP
    random_part = jax.random.randint(block_key, (device_count, slot_count), 0, 16384)
    slot_score = (owner_bias[slot_owner][None, :] + random_part) * slot_count + jnp.arange(slot_count)[None, :]
    _, chosen = lax.top_k(slot_score, 2 * ROWS)
    shuffle_keys = jax.random.split(order_key, device_count)
    chosen = jax.vmap(jax.random.permutation)(shuffle_keys, chosen)
    owner = (chosen // CAP).reshape(device_count, ROWS, 2)
    owner_dp = owner // N_LIST
    owner_list = owner % N_LIST
    list_pick = jax.random.randint(list_key, (device_count, ROWS, 2), 0, per_owner)
    collide = (owner[..., 0] == owner[..., 1]) & (list_pick[..., 0] == list_pick[..., 1])
    second = jnp.where(collide, (list_pick[..., 1] + 1) % per_owner, list_pick[..., 1])
    list_pick = jnp.stack([list_pick[..., 0], second], axis=-1)
    identity = owner_list * per_device + list_pick * N_DP + owner_dp
    return identity.reshape(device_count * ROWS, 2).astype(jnp.int32)


def steps_of(own_key, dims, shards, least, top_value):
    def one(dim, shards_of):
        draws = jax.random.uniform(jax.random.fold_in(jax.random.fold_in(own_key, 6), dim), (shards_of,), jnp.float32, least / len(shards), top_value / len(shards))
        return jnp.repeat(jnp.exp(draws), dims[dim] // shards_of).reshape((-1,) + (1,) * (len(dims) - dim - 1))

    level = one(*shards[0])
    for cut in shards[1:]:
        level = level * one(*cut)
    return level


def scatter_about(rng, extent, spread, reach, cuts=(), kind=jnp.bfloat16):
    level = steps_of(rng, extent, cuts, -0.22, 0.18) if cuts else 1.0
    drawn = jax.random.normal(rng, extent, jnp.float32) * spread * level
    return jnp.minimum(jnp.maximum(drawn, -reach), reach).astype(kind)


def setup_inputs(seed: int = 0) -> dict:
    key_list = jax.random.split(jax.random.key(seed), 5)
    vectors = scatter_about(key_list[0], (VECTORS, D), 1.0, 6.0, ((0, 128),))
    centroids = scatter_about(key_list[1], (LISTS, D), 1.0, 6.0, ((0, 16),))
    projection = scatter_about(key_list[2], (D, PDIM), D ** -0.5, 0.21875)
    list_ids = draw_list_ids(jax.random.fold_in(key_list[4], 71), 0)
    return {"vectors": vectors, "centroids": centroids, "projection": projection, "list_ids": list_ids}


soar_weight = 1.5
masked_score = 1.0e30


def reference(vectors, centroids, projection, list_ids):
    per_device = LISTS // N_LIST
    device_count = N_DP * N_LIST
    primary = list_ids[:, 0]
    head_prefix = vectors[:, :PREFIX]
    primary_prefix = centroids[primary, :PREFIX]
    residual = (head_prefix.astype(jnp.float32) - primary_prefix.astype(jnp.float32)).astype(jnp.bfloat16)
    head_float = head_prefix.astype(jnp.float32)
    resid_float = residual.astype(jnp.float32)
    head_square = jnp.sum(head_float * head_float, axis=1)
    cross_term = jnp.sum(resid_float * head_float, axis=1)
    resid_power = jnp.mean(resid_float * resid_float, axis=1) + 1.0e-6
    block_size = min(512, LISTS)
    block_total = LISTS // block_size
    blocks = centroids[:, :PREFIX].reshape(block_total, block_size, PREFIX)

    def sweep_block(lowest, inputs):
        block_index, block = inputs
        block_float = block.astype(jnp.float32)
        block_square = jnp.sum(block_float * block_float, axis=1)
        dot_head = jnp.dot(head_prefix, block.T, preferred_element_type=jnp.float32)
        dot_resid = jnp.dot(residual, block.T, preferred_element_type=jnp.float32)
        distance = head_square[:, None] - 2.0 * dot_head + block_square[None, :]
        along = cross_term[:, None] - dot_resid
        scores = (distance + soar_weight * along * along / (PREFIX * resid_power[:, None])) / PREFIX
        list_global = block_index * block_size + jnp.arange(block_size, dtype=jnp.int32)
        scores = jnp.where(list_global[None, :] == primary[:, None], masked_score, scores)
        return jnp.minimum(lowest, jnp.min(scores, axis=1)), None

    start_value = jnp.full((VECTORS,), masked_score, jnp.float32)
    lowest_score, _ = lax.scan(sweep_block, start_value, (jnp.arange(block_total, dtype=jnp.int32), blocks))

    projected = jnp.dot(vectors, projection, preferred_element_type=jnp.float32).astype(jnp.bfloat16)
    flat_ids = list_ids.reshape(-1)
    owner_index = (flat_ids % N_DP) * N_LIST + flat_ids // per_device
    owner_blocks = owner_index.reshape(device_count, 2 * ROWS)
    one_hot = (owner_blocks[:, :, None] == jnp.arange(device_count, dtype=jnp.int32)[None, None, :]).astype(jnp.int32)
    slot_rank = jnp.sum(one_hot * (jnp.cumsum(one_hot, axis=1) - 1), axis=2).reshape(-1)
    source = jnp.arange(2 * VECTORS, dtype=jnp.int32) // (2 * ROWS)
    position = owner_index * (device_count * CAP) + source * CAP + slot_rank
    centroid_proj = jnp.dot(centroids[flat_ids], projection, preferred_element_type=jnp.float32)
    doubled = jnp.repeat(projected, 2, axis=0).astype(jnp.float32)
    values = (doubled - centroid_proj).astype(jnp.bfloat16)
    placed = jnp.zeros((device_count * device_count * CAP, PDIM), jnp.bfloat16).at[position].set(values)
    return placed, lowest_score
```

```python
import functools

import jax
import jax.numpy as jnp
from jax import lax
from jax.experimental import pallas as pl
from jax.experimental.pallas import tpu as pltpu
from jax.sharding import PartitionSpec as P

PREFIX = 256
N_DP = 8
N_LIST = 16
SIDE = 4
ROWS = 256
HALF = 128
LISTS = 4096
CAP = 8
SLOTS = N_DP * CAP
PDIM = 128

soar_weight = 1.5
masked_score = 1e30
NT = (((1,), (1,)), ((), ()))
bf16 = jnp.bfloat16
f32 = jnp.float32
i32 = jnp.int32


def iota(shape, dim):
    return lax.broadcasted_iota(i32, shape, dim)


def ones_where(mask):
    return jnp.where(mask, 1.0, 0.0)


def dot(a, b):
    return jnp.dot(a, b, preferred_element_type=f32)


def params(mib):
    return pltpu.CompilerParams(vmem_limit_bytes=mib << 20)


def split3(x):
    hi = x.astype(bf16)
    rest = x - hi.astype(f32)
    mid = rest.astype(bf16)
    low = (rest - mid.astype(f32)).astype(bf16)
    return hi, mid, low


def to_column(row, n):
    eye = iota((n, n), 0) == iota((n, n), 1)
    return jnp.sum(jnp.where(eye, jnp.broadcast_to(row, (n, n)), 0.0), axis=1, keepdims=True)


def to_row(column, n):
    eye = iota((n, n), 0) == iota((n, n), 1)
    return jnp.sum(jnp.where(eye, jnp.broadcast_to(column, (n, n)), 0.0), axis=0, keepdims=True)


def pack_kernel(place, ids_ref, c_ref, out_ref):
    list_place = place[1]
    ids = ids_ref[0]
    inside = (ids >> 12) == list_place
    upto = ones_where(iota((ROWS, ROWS), 0) <= iota((ROWS, ROWS), 1)).astype(bf16)
    count = dot(ones_where(inside).astype(bf16), upto)
    rank = jnp.where(inside, count - 1.0, -1.0)
    local = (ids & (LISTS - 1)).astype(f32) + 1.0
    slot = iota((SLOTS, ROWS), 0).astype(f32)
    lane = iota((4 * SLOTS, LISTS), 1).astype(f32)
    for g in range(N_LIST // 4):
        picks = []
        for s in range(4 * g, 4 * g + 4):
            hit = slot == rank[s : s + 1, :]
            picks.append(jnp.sum(jnp.where(hit, local[s : s + 1, :], 0.0), axis=1, keepdims=True))
        pick = jnp.concatenate(picks, axis=0) - 1.0
        hot = ones_where(lane == pick).astype(bf16)
        out_ref[4 * g : 4 * g + 4] = (
            dot(hot, c_ref[...]).astype(bf16).reshape(4, SLOTS, PREFIX)
        )


def pack(place, ids, centroids):
    return pl.pallas_call(
        pack_kernel,
        out_shape=jax.ShapeDtypeStruct((N_LIST, SLOTS, PREFIX), bf16),
        grid_spec=pltpu.PrefetchScalarGridSpec(
            num_scalar_prefetch=1,
            grid=(1,),
            in_specs=[
                pl.BlockSpec((1, N_LIST, ROWS), lambda i, p: (0, p[0], 0)),
                pl.BlockSpec((LISTS, PREFIX), lambda i, p: (0, 0)),
            ],
            out_specs=pl.BlockSpec((N_LIST, SLOTS, PREFIX), lambda i, p: (0, 0, 0)),
        ),
        compiler_params=params(40),
        name="pack_prefixes",
    )(place, ids, centroids)


def residual_kernel(place, ids_ref, got_ref, head_ref, resid_ref, square_ref):
    own = place[1]
    ids = ids_ref[0, pl.ds(own, 1), :]
    shard = ids >> 12
    member = iota((N_LIST, ROWS), 0) == shard
    upto = ones_where(iota((ROWS, ROWS), 0) <= iota((ROWS, ROWS), 1)).astype(bf16)
    count = dot(ones_where(member).astype(bf16), upto)
    rank = jnp.sum(jnp.where(member, count - 1.0, 0.0), axis=0, keepdims=True)
    slot = to_column((shard * SLOTS).astype(f32) + rank, ROWS)
    hot = ones_where(iota((ROWS, N_LIST * SLOTS), 1).astype(f32) == slot).astype(bf16)
    primary = dot(hot, got_ref[...].reshape(N_LIST * SLOTS, PREFIX))
    head = head_ref[...].astype(f32)
    resid = (head - primary).astype(bf16).astype(f32)
    power = jnp.sum(resid * resid, axis=1, keepdims=True) * (1.0 / PREFIX) + 1e-6
    scale = jnp.sqrt(soar_weight / (PREFIX * power))
    resid_ref[...] = (resid * scale).astype(bf16)
    square_ref[...] = to_row(jnp.sum(head * head, axis=1, keepdims=True), ROWS)


def residuals(place, ids, got, vectors):
    return pl.pallas_call(
        residual_kernel,
        out_shape=(
            jax.ShapeDtypeStruct((ROWS, PREFIX), bf16),
            jax.ShapeDtypeStruct((1, ROWS), f32),
        ),
        grid_spec=pltpu.PrefetchScalarGridSpec(
            num_scalar_prefetch=1,
            grid=(1,),
            in_specs=[
                pl.BlockSpec((1, N_LIST, ROWS), lambda i, p: (0, p[0], 0)),
                pl.BlockSpec((N_LIST, SLOTS, PREFIX), lambda i, p: (0, 0, 0)),
                pl.BlockSpec((ROWS, PREFIX), lambda i, p: (0, 0)),
            ],
            out_specs=(
                pl.BlockSpec((ROWS, PREFIX), lambda i, p: (0, 0)),
                pl.BlockSpec((1, ROWS), lambda i, p: (0, 0)),
            ),
        ),
        compiler_params=params(32),
        name="own_residuals",
    )(place, ids, got, vectors)


def owned_kernel(place, c_ref, proj_ref, hi_ref, mid_ref, low_ref, square_ref):
    mine = place[0]
    c = c_ref[...]
    rows = c.shape[0]
    full = dot(c, proj_ref[...]).reshape(rows // N_DP, N_DP, PDIM)
    keep = iota((rows // N_DP, N_DP, PDIM), 1) == mine
    owned = jnp.sum(jnp.where(keep, full, 0.0), axis=1)
    hi_ref[...], mid_ref[...], low_ref[...] = split3(owned)
    head = c[:, :PREFIX].astype(f32)
    square = head * head
    upper = square.astype(bf16)
    lower = (square - upper.astype(f32)).astype(bf16)
    one = jnp.ones((PREFIX, 128), bf16)
    square_ref[...] = dot(upper, one) + dot(lower, one)


def owned(place, centroids, projection):
    block = 1024
    part = jax.ShapeDtypeStruct((LISTS // N_DP, PDIM), bf16)
    part_spec = pl.BlockSpec((block // N_DP, PDIM), lambda i, p: (i, 0))
    return pl.pallas_call(
        owned_kernel,
        out_shape=(part, part, part, jax.ShapeDtypeStruct((LISTS, 128), f32)),
        grid_spec=pltpu.PrefetchScalarGridSpec(
            num_scalar_prefetch=1,
            grid=(LISTS // block,),
            in_specs=[
                pl.BlockSpec((block, centroids.shape[1]), lambda i, p: (i, 0)),
                pl.BlockSpec(projection.shape, lambda i, p: (0, 0)),
            ],
            out_specs=(
                part_spec,
                part_spec,
                part_spec,
                pl.BlockSpec((block, 128), lambda i, p: (i, 0)),
            ),
        ),
        compiler_params=params(32),
        name="owned_projection",
    )(place, centroids, projection)


def rank_tables(first, second):
    before = ones_where(iota((ROWS, ROWS), 0) < iota((ROWS, ROWS), 1)).astype(bf16)
    one0, one1 = ones_where(first), ones_where(second)
    earlier = dot((one0 + one1).astype(bf16), before)
    return jnp.where(first, earlier, -1.0), jnp.where(second, earlier + one0, -1.0)


def eightfold(table):
    n = table.shape[0]
    return jnp.broadcast_to(table[:, None, :], (n, CAP, ROWS)).reshape(n * CAP, ROWS)


def send_kernel(place, id0_ref, id1_ref, vec_ref, proj_ref, out_ref):
    own = place[1]
    devices = N_DP * N_LIST
    hits = []
    for ref in (id0_ref, id1_ref):
        ids = ref[0, pl.ds(own, 1), :]
        hits.append(iota((devices, ROWS), 0) == (ids & (N_DP - 1)) * N_LIST + (ids >> 12))
    rank0, rank1 = rank_tables(*hits)
    slot = (iota((devices * CAP, ROWS), 0) & (CAP - 1)).astype(f32)
    hot = ones_where((eightfold(rank0) == slot) | (eightfold(rank1) == slot)).astype(bf16)
    payload = dot(vec_ref[...], proj_ref[...]).astype(bf16)
    out_ref[...] = dot(hot, payload).astype(bf16).reshape(devices, CAP, PDIM)


def outgoing(place, ids, vectors, projection):
    devices = N_DP * N_LIST
    return pl.pallas_call(
        send_kernel,
        out_shape=jax.ShapeDtypeStruct((devices, CAP, PDIM), bf16),
        grid_spec=pltpu.PrefetchScalarGridSpec(
            num_scalar_prefetch=1,
            grid=(1,),
            in_specs=[
                pl.BlockSpec((1, N_LIST, ROWS), lambda i, p: (0, p[0], 0)),
                pl.BlockSpec((1, N_LIST, ROWS), lambda i, p: (1, p[0], 0)),
                pl.BlockSpec(vectors.shape, lambda i, p: (0, 0)),
                pl.BlockSpec(projection.shape, lambda i, p: (0, 0)),
            ],
            out_specs=pl.BlockSpec((devices, CAP, PDIM), lambda i, p: (0, 0, 0)),
        ),
        compiler_params=params(32),
        name="outgoing_rows",
    )(place, ids, ids, vectors, projection)


def place_kernel(place, ids_ref, got_ref, hi_ref, mid_ref, low_ref, out_ref):
    devices = N_DP * N_LIST
    id0, id1 = ids_ref[0], ids_ref[1]
    hits, local = [], []
    for ids in (id0, id1):
        hits.append(((ids & (N_DP - 1)) == place[0]) & ((ids >> 12) == place[1]))
        local.append(((ids & (LISTS - 1)) >> 3).astype(f32) + 1.0)
    rank0, rank1 = rank_tables(*hits)
    slot = (iota((devices * CAP, ROWS), 0) & (CAP - 1)).astype(f32)
    pick = jnp.where(eightfold(rank0) == slot, eightfold(local[0]), 0.0)
    pick += jnp.where(eightfold(rank1) == slot, eightfold(local[1]), 0.0)
    pick = jnp.sum(pick, axis=1, keepdims=True) - 1.0
    per_owner = LISTS // N_DP
    hot = ones_where(iota((devices * CAP, per_owner), 1).astype(f32) == pick).astype(bf16)
    centroid = dot(hot, hi_ref[...]) + dot(hot, mid_ref[...]) + dot(hot, low_ref[...])
    got = got_ref[...].reshape(devices * CAP, PDIM).astype(f32)
    out_ref[...] = jnp.where(pick >= 0.0, got - centroid, 0.0).astype(bf16)


def placement(place, ids, got, parts):
    devices = N_DP * N_LIST
    part_spec = pl.BlockSpec(parts[0].shape, lambda i, p: (0, 0))
    return pl.pallas_call(
        place_kernel,
        out_shape=jax.ShapeDtypeStruct((devices * CAP, PDIM), bf16),
        grid_spec=pltpu.PrefetchScalarGridSpec(
            num_scalar_prefetch=1,
            grid=(1,),
            in_specs=[
                pl.BlockSpec(ids.shape, lambda i, p: (0, 0, 0)),
                pl.BlockSpec(got.shape, lambda i, p: (0, 0, 0)),
                part_spec,
                part_spec,
                part_spec,
            ],
            out_specs=pl.BlockSpec((devices * CAP, PDIM), lambda i, p: (0, 0)),
        ),
        compiler_params=params(32),
        name="place_rows",
    )(place, ids, got, *parts)


def score_kernel(halves, n_arrays, has_last, place, *refs):
    ids_ref, c_hbm, square_hbm = refs[:3]
    arrays = refs[3 : 3 + n_arrays]
    rest = refs[3 + n_arrays :]
    last_ref = rest[0] if has_last else None
    out_ref, c_ref, square_ref, head_ref, resid_ref, prim_ref, low_ref, sems = rest[has_last:]
    tiles = len(halves) // 2
    own = place[1]
    copies = [
        pltpu.make_async_copy(c_hbm.at[:, pl.ds(0, PREFIX)], c_ref, sems.at[0]),
        pltpu.make_async_copy(square_hbm, square_ref, sems.at[1]),
    ]
    sources = []
    for n, (h_at, h_row, r_at, r_row, dy, dz, half) in enumerate(halves):
        to = pl.ds(n * HALF, HALF)
        copies.append(
            pltpu.make_async_copy(
                arrays[h_at].at[pl.ds(h_row, HALF), pl.ds(0, PREFIX)], head_ref.at[to], sems.at[2 + 2 * n]
            )
        )
        copies.append(
            pltpu.make_async_copy(
                arrays[r_at].at[pl.ds(r_row, HALF), pl.ds(0, PREFIX)], resid_ref.at[to], sems.at[3 + 2 * n]
            )
        )
        y = (own // SIDE + SIDE - dy) % SIDE
        z = (own % SIDE + SIDE - dz) % SIDE
        sources.append(y * SIDE + z)
    for copy in copies:
        copy.start()
    for n, half in enumerate(halves):
        row = ids_ref[0, pl.ds(sources[n], 1), :] - own * LISTS
        prim_ref[n // 2 : n // 2 + 1, (n % 2) * HALF : (n % 2 + 1) * HALF] = row[
            :, half[6] * HALF : (half[6] + 1) * HALF
        ]
    for copy in copies:
        copy.wait()
    eye = iota((ROWS, ROWS), 0) == iota((ROWS, ROWS), 1)
    number = iota((LISTS, ROWS), 0)

    def one_tile(tile, carry):
        at = pl.multiple_of(tile * ROWS, ROWS)
        head = head_ref[pl.ds(at, ROWS), :]
        resid = resid_ref[pl.ds(at, ROWS), :]
        both = lax.dot_general(head, resid, NT, preferred_element_type=f32)
        cross = jnp.sum(jnp.where(eye, both, 0.0), axis=0, keepdims=True)
        dot_head = lax.dot_general(c_ref[...], head * bf16(-2), NT, preferred_element_type=f32)
        dot_resid = lax.dot_general(c_ref[...], resid, NT, preferred_element_type=f32)
        square = square_ref[...]
        square = jnp.concatenate([square, square], axis=1)
        along = cross - dot_resid
        score = (dot_head + square) + along * along
        score = jnp.where(number == prim_ref[pl.ds(tile, 1), :], masked_score, score)
        low_ref[pl.ds(tile, 1), :] = jnp.min(
            jnp.min(score.reshape(LISTS // 8, 8, ROWS), axis=0), axis=0, keepdims=True
        )
        return carry

    lax.fori_loop(0, tiles, one_tile, 0, unroll=2)
    result = last_ref[...] if has_last else jnp.zeros(out_ref.shape, f32)
    row = iota(result.shape, 0)
    side = iota(result.shape, 1) // HALF
    for n, half in enumerate(halves):
        low = low_ref[n // 2 : n // 2 + 1, (n % 2) * HALF : (n % 2 + 1) * HALF]
        low = jnp.broadcast_to(jnp.concatenate([low, low], axis=1), result.shape)
        result = jnp.where((row == sources[n]) & (side == half[6]), low, result)
    out_ref[...] = result


def scores(name, place, ids, centroids, square, arrays, halves, last=None):
    rows = len(halves) * HALF
    has_last = last is not None
    low_spec = pl.BlockSpec((N_LIST, ROWS), lambda i, p: (0, 0))
    return pl.pallas_call(
        functools.partial(score_kernel, halves, len(arrays), has_last),
        out_shape=jax.ShapeDtypeStruct((N_LIST, ROWS), f32),
        grid_spec=pltpu.PrefetchScalarGridSpec(
            num_scalar_prefetch=1,
            grid=(1,),
            in_specs=[pl.BlockSpec((1, N_LIST, ROWS), lambda i, p: (0, p[0], 0))]
            + [pl.BlockSpec(memory_space=pl.ANY)] * (2 + len(arrays))
            + [low_spec] * has_last,
            out_specs=low_spec,
            scratch_shapes=[
                pltpu.VMEM((LISTS, PREFIX), bf16),
                pltpu.VMEM((LISTS, 128), f32),
                pltpu.VMEM((rows, PREFIX), bf16),
                pltpu.VMEM((rows, PREFIX), bf16),
                pltpu.VMEM((max(8, rows // ROWS), ROWS), i32),
                pltpu.VMEM((max(8, rows // ROWS), ROWS), f32),
                pltpu.SemaphoreType.DMA((2 + 2 * len(halves),)),
            ],
        ),
        compiler_params=params(40),
        name=name,
    )(place, ids, centroids, square, *arrays, *([last] if has_last else []))


def final_kernel(got_ref, square_ref, out_ref):
    low = jnp.min(got_ref[...], axis=0, keepdims=True)
    out_ref[...] = (low + square_ref[...]) * (1.0 / PREFIX)


def step(dy, dz):
    pairs = []
    for at in range(N_LIST):
        y, z = divmod(at, SIDE)
        pairs.append((at, (y + dy) % SIDE * SIDE + (z + dz) % SIDE))
    return pairs


def shift(x, dy, dz):
    return lax.ppermute(x, "list", step(dy, dz))


def local(vectors, centroids, projection, list_ids):
    place = jnp.stack([lax.axis_index("dp"), lax.axis_index("list")]).astype(i32)
    ids = list_ids.T.reshape(2, N_DP * N_LIST, ROWS)
    head = vectors[:, :PREFIX]

    head_z = [head] + [shift(head, 0, dz) for dz in range(1, SIDE)]
    head_row = jnp.concatenate(head_z, axis=0)
    head_y = [None] + [shift(head_row, dy, 0) for dy in range(1, SIDE)]

    slots = pack(place, ids, centroids)
    got = lax.all_to_all(slots, "list", 0, 0, tiled=True)
    resid, head_square = residuals(place, ids, got, vectors)

    low, high = resid[:HALF], resid[HALF:]
    low_z = [low] + [shift(low, 0, dz) for dz in range(1, SIDE)]
    high_y = [high] + [shift(high, dy, 0) for dy in range(1, SIDE)]
    low_row = jnp.concatenate(low_z, axis=0)
    high_column = jnp.concatenate(high_y, axis=0)
    low_zy = [None] + [shift(low_row, dy, 0) for dy in range(1, SIDE)]
    high_yz = [None] + [shift(high_column, 0, dz) for dz in range(1, SIDE)]

    rows_out = outgoing(place, ids, vectors, projection)
    rows_in = lax.all_to_all(rows_out, ("dp", "list"), 0, 0, tiled=True)
    *parts, square = owned(place, centroids, projection)
    placed = placement(place, ids, rows_in, parts)

    arrays = [vectors, *head_z[1:], *head_y[1:]]

    def head_of(dy, dz, half):
        if dy == 0:
            return dz, half * HALF
        return SIDE - 1 + dy, dz * ROWS + half * HALF

    def call(name, given, blocks, last=None):
        used, halves = [], []
        for r_array, r_row, dy, dz, half in blocks:
            h_at, h_row = head_of(dy, dz, half)
            spots = []
            for x in (arrays[h_at], r_array):
                known = [n for n, y in enumerate(used) if y is x]
                if not known:
                    used.append(x)
                    known = [len(used) - 1]
                spots.append(known[0])
            halves.append((spots[0], h_row, spots[1], r_row, dy, dz, half))
        return scores(name, place, ids, centroids, square, used, tuple(halves), last)

    near = [(low, 0, 0, 0, 0), (high, 0, 0, 0, 1)]
    near += [(low_z[dz], 0, 0, dz, 0) for dz in range(1, SIDE)]
    near += [(high_y[dy], 0, dy, 0, 1) for dy in range(1, SIDE)]

    def far(d):
        blocks = [(low_zy[d], dz * HALF, d, dz, 0) for dz in range(SIDE)]
        return blocks + [(high_yz[d], dy * HALF, dy, d, 1) for dy in range(SIDE)]

    lowest = call("scores_near", arrays, near)
    lowest = call("scores_next", arrays, far(1) + far(3), lowest)
    lowest = call("scores_far", arrays, far(2), lowest)
    back = lax.all_to_all(lowest, "list", 0, 0, tiled=True)
    lowest_score = pl.pallas_call(
        final_kernel, out_shape=jax.ShapeDtypeStruct((1, ROWS), f32), name="lowest"
    )(back, head_square)
    return placed, lowest_score.reshape(ROWS)


def solution(mesh):
    return jax.shard_map(
        local,
        mesh=mesh,
        in_specs=(P(("dp", "list"), None), P("list", None), P(), P()),
        out_specs=(P(("dp", "list"), None), P(("dp", "list"))),
        check_vma=False,
    )
```

```python
import functools

import jax
import jax.numpy as jnp
from jax import lax
from jax.experimental import pallas as pl
from jax.experimental.pallas import tpu as pltpu
from jax.sharding import PartitionSpec as P

PREFIX = 256
N_DP = 8
N_LIST = 16
SIDE = 4
ROWS = 256
HALF = 128
LISTS = 4096
CAP = 8
SLOTS = N_DP * CAP
PDIM = 128

soar_weight = 1.5
masked_score = 1e30
NT = (((1,), (1,)), ((), ()))
bf16 = jnp.bfloat16
f32 = jnp.float32
i32 = jnp.int32


def iota(shape, dim):
    return lax.broadcasted_iota(i32, shape, dim)


def ones_where(mask):
    return jnp.where(mask, 1.0, 0.0)


def dot(a, b):
    return jnp.dot(a, b, preferred_element_type=f32)


def params(mib):
    return pltpu.CompilerParams(vmem_limit_bytes=mib << 20)


def split3(x):
    hi = x.astype(bf16)
    rest = x - hi.astype(f32)
    mid = rest.astype(bf16)
    low = (rest - mid.astype(f32)).astype(bf16)
    return hi, mid, low


def to_column(row, n):
    eye = iota((n, n), 0) == iota((n, n), 1)
    return jnp.sum(jnp.where(eye, jnp.broadcast_to(row, (n, n)), 0.0), axis=1, keepdims=True)


def to_row(column, n):
    eye = iota((n, n), 0) == iota((n, n), 1)
    return jnp.sum(jnp.where(eye, jnp.broadcast_to(column, (n, n)), 0.0), axis=0, keepdims=True)


VMEM = pl.BlockSpec(memory_space=pltpu.VMEM)
HBM = pl.BlockSpec(memory_space=pltpu.HBM)


def places():
    return lax.axis_index("dp"), lax.axis_index("list")


def call(kernel, name, mib, out_shape, *operands, hbm=(), scratch=()):
    return pl.pallas_call(
        kernel,
        out_shape=out_shape,
        in_specs=[HBM if n in hbm else VMEM for n in range(len(operands))],
        out_specs=jax.tree.map(lambda _: VMEM, out_shape),
        scratch_shapes=scratch,
        compiler_params=params(mib),
        name=name,
    )(*operands)


def pack_kernel(ids_ref, c_ref, out_ref):
    group, list_place = places()
    upto = ones_where(iota((ROWS, ROWS), 0) <= iota((ROWS, ROWS), 1)).astype(bf16)
    base = group * (N_LIST * ROWS)
    ids = jnp.concatenate(
        [
            ids_ref[0:1, pl.ds(pl.multiple_of(base + s * ROWS, ROWS), ROWS)]
            for s in range(N_LIST)
        ],
        axis=0,
    )
    inside = (ids >> 12) == list_place
    count = dot(ones_where(inside).astype(bf16), upto)
    rank = jnp.where(inside, count - 1.0, -1.0)
    local = (ids & (LISTS - 1)).astype(f32) + 1.0
    slot = iota((SLOTS, ROWS), 0).astype(f32)
    lane = iota((4 * SLOTS, LISTS), 1).astype(f32)
    for g in range(N_LIST // 4):
        picks = []
        for s in range(4 * g, 4 * g + 4):
            hit = slot == rank[s : s + 1, :]
            picks.append(jnp.sum(jnp.where(hit, local[s : s + 1, :], 0.0), axis=1, keepdims=True))
        pick = jnp.concatenate(picks, axis=0) - 1.0
        hot = ones_where(lane == pick).astype(bf16)
        out_ref[4 * g : 4 * g + 4] = (
            dot(hot, c_ref[...]).astype(bf16).reshape(4, SLOTS, PREFIX)
        )


def pack(ids, prefixes):
    shape = jax.ShapeDtypeStruct((N_LIST, SLOTS, PREFIX), bf16)
    return call(pack_kernel, "pack_prefixes", 16, shape, ids, prefixes)


def residual_kernel(
    ids_ref, got_ref, vec_hbm, keep_ref, send_ref, square_ref, head_ref, resid_ref, sem
):
    group, own = places()
    fetch = pltpu.make_async_copy(vec_hbm.at[:, pl.ds(0, PREFIX)], head_ref, sem)
    fetch.start()
    at = pl.multiple_of((group * N_LIST + own) * ROWS, ROWS)
    shard = ids_ref[0:1, pl.ds(at, ROWS)] >> 12
    member = iota((N_LIST, ROWS), 0) == shard
    upto = ones_where(iota((ROWS, ROWS), 0) <= iota((ROWS, ROWS), 1)).astype(bf16)
    count = dot(ones_where(member).astype(bf16), upto)
    rank = jnp.sum(jnp.where(member, count - 1.0, 0.0), axis=0, keepdims=True)
    slot = to_column((shard * SLOTS).astype(f32) + rank, ROWS)
    hot = ones_where(iota((ROWS, N_LIST * SLOTS), 1).astype(f32) == slot).astype(bf16)
    primary = dot(hot, got_ref[...].reshape(N_LIST * SLOTS, PREFIX))
    fetch.wait()
    head = head_ref[...].astype(f32)
    resid = (head - primary).astype(bf16).astype(f32)
    power = jnp.sum(resid * resid, axis=1, keepdims=True) * (1.0 / PREFIX) + 1e-6
    scale = jnp.sqrt(soar_weight / (PREFIX * power))
    resid_ref[...] = (resid * scale).astype(bf16)
    square_ref[...] = to_row(jnp.sum(head * head, axis=1, keepdims=True), ROWS)
    core = group % 2
    for half, to in ((core, keep_ref), (1 - core, send_ref)):
        rows = pl.ds(pl.multiple_of(half * HALF, HALF), HALF)
        to[:HALF] = head_ref[rows, :]
        to[HALF:] = resid_ref[rows, :]


def residuals(ids, got, vectors):
    halves = jax.ShapeDtypeStruct((2 * HALF, PREFIX), bf16)
    shape = (halves, halves, jax.ShapeDtypeStruct((1, ROWS), f32))
    scratch = [pltpu.VMEM((ROWS, PREFIX), bf16)] * 2 + [pltpu.SemaphoreType.DMA]
    return call(
        residual_kernel, "own_residuals", 8, shape, ids, got, vectors, hbm=(2,), scratch=scratch
    )


def rank_tables(first, second):
    before = ones_where(iota((ROWS, ROWS), 0) < iota((ROWS, ROWS), 1)).astype(bf16)
    one0, one1 = ones_where(first), ones_where(second)
    earlier = dot((one0 + one1).astype(bf16), before)
    return jnp.where(first, earlier, -1.0), jnp.where(second, earlier + one0, -1.0)


def eightfold(table):
    n = table.shape[0]
    return jnp.broadcast_to(table[:, None, :], (n, CAP, ROWS)).reshape(n * CAP, ROWS)


def prepare_kernel(
    ids_ref, c_hbm, vec_hbm, proj_ref, rows_ref, parts_ref, c_ref, vec_ref, sems
):
    group, own = places()
    step_rows = LISTS // 8
    wide = pltpu.make_async_copy(vec_hbm, vec_ref, sems.at[8])
    wide.start()
    copies = [
        pltpu.make_async_copy(
            c_hbm.at[pl.ds(n * step_rows, step_rows)],
            c_ref.at[pl.ds(n * step_rows, step_rows)],
            sems.at[n],
        )
        for n in range(8)
    ]
    for copy in copies:
        copy.start()
    at = pl.multiple_of((group * N_LIST + own) * ROWS, ROWS)
    devices = N_DP * N_LIST
    hits = []
    for k in range(2):
        ids = ids_ref[k : k + 1, pl.ds(at, ROWS)]
        hits.append(iota((devices, ROWS), 0) == (ids & (N_DP - 1)) * N_LIST + (ids >> 12))
    rank0, rank1 = rank_tables(*hits)
    slot = (iota((devices * CAP, ROWS), 0) & (CAP - 1)).astype(f32)
    hot = ones_where((eightfold(rank0) == slot) | (eightfold(rank1) == slot)).astype(bf16)
    wide.wait()
    payload = dot(vec_ref[...], proj_ref[...]).astype(bf16)
    rows_ref[...] = dot(hot, payload).astype(bf16).reshape(devices, CAP, PDIM)
    per = step_rows // N_DP
    chosen = iota((per, step_rows), 1) == N_DP * iota((per, step_rows), 0) + group
    chosen = ones_where(chosen).astype(bf16)
    for n, copy in enumerate(copies):
        copy.wait()
        mine = dot(chosen, c_ref[n * step_rows : (n + 1) * step_rows]).astype(bf16)
        for k, part in enumerate(split3(dot(mine, proj_ref[...]))):
            parts_ref[k, n * per : (n + 1) * per] = part


def prepare(ids, centroids, vectors, projection):
    shape = (
        jax.ShapeDtypeStruct((N_DP * N_LIST, CAP, PDIM), bf16),
        jax.ShapeDtypeStruct((3, LISTS // N_DP, PDIM), bf16),
    )
    scratch = [
        pltpu.VMEM(centroids.shape, bf16),
        pltpu.VMEM(vectors.shape, bf16),
        pltpu.SemaphoreType.DMA((9,)),
    ]
    return call(
        prepare_kernel, "prepare_rows", 56, shape, ids, centroids, vectors, projection, hbm=(1, 2), scratch=scratch
    )


def place_kernel(ids_ref, got_ref, parts_ref, out_ref):
    group, own = places()
    devices = N_DP * N_LIST
    hits, local = [], []
    for k in range(2):
        ids = ids_ref[k]
        hits.append(((ids & (N_DP - 1)) == group) & ((ids >> 12) == own))
        local.append(((ids & (LISTS - 1)) >> 3).astype(f32) + 1.0)
    rank0, rank1 = rank_tables(*hits)
    slot = (iota((devices * CAP, ROWS), 0) & (CAP - 1)).astype(f32)
    pick = jnp.where(eightfold(rank0) == slot, eightfold(local[0]), 0.0)
    pick += jnp.where(eightfold(rank1) == slot, eightfold(local[1]), 0.0)
    pick = jnp.sum(pick, axis=1, keepdims=True) - 1.0
    per_owner = LISTS // N_DP
    hot = ones_where(iota((devices * CAP, per_owner), 1).astype(f32) == pick).astype(bf16)
    centroid = dot(hot, parts_ref[0]) + dot(hot, parts_ref[1]) + dot(hot, parts_ref[2])
    got = got_ref[...].reshape(devices * CAP, PDIM).astype(f32)
    out_ref[...] = jnp.where(pick >= 0.0, got - centroid, 0.0).astype(bf16)


def placement(ids, got, parts):
    shape = jax.ShapeDtypeStruct((N_DP * N_LIST * CAP, PDIM), bf16)
    return call(place_kernel, "place_rows", 12, shape, ids, got, parts)


def squares_of(rows):
    square = jnp.square(rows.astype(f32))
    upper = square.astype(bf16)
    lower = (square - upper.astype(f32)).astype(bf16)
    one = jnp.ones((PREFIX, 128), bf16)
    return dot(upper, one) + dot(lower, one)


def score_kernel(steps, n_arrays, given, *refs):
    ids_ref, c_ref = refs[:2]
    arrays = refs[2 : 2 + n_arrays]
    rest = refs[2 + n_arrays :]
    if given == 2:
        square_ref, out_ref = rest[1:]
    else:
        out_ref, square_ref = rest[given:]
        square_ref[...] = squares_of(c_ref[...])
    out_ref[...] = rest[0][...] if given else jnp.zeros(out_ref.shape, f32)
    group, own = places()
    core = group % 2
    eye = iota((ROWS, ROWS), 0) == iota((ROWS, ROWS), 1)
    number = iota((LISTS, ROWS), 0)
    for n, (one, two) in enumerate(steps):
        dy = two + core * (one - two)
        dz = one + core * (two - one)
        spot = (own // SIDE + SIDE - dy) % SIDE * SIDE + (own % SIDE + SIDE - dz) % SIDE
        prims = []
        for k in range(2):
            device = (group + k * (1 - 2 * core)) * N_LIST + spot
            lane = pl.multiple_of(device * ROWS + core * HALF, HALF)
            prims.append(ids_ref[0:1, pl.ds(lane, HALF)] - own * LISTS)
        prim = jnp.concatenate(prims, axis=1)
        each = SIDE // n_arrays
        ref, at = arrays[n // each], n % each * 2 * ROWS
        parts = [ref[at + k * HALF : at + (k + 1) * HALF] for k in range(4)]
        head = jnp.concatenate([parts[0], parts[2]], axis=0)
        resid = jnp.concatenate([parts[1], parts[3]], axis=0)
        both = lax.dot_general(head, resid, NT, preferred_element_type=f32)
        cross = jnp.sum(jnp.where(eye, both, 0.0), axis=0, keepdims=True)
        dot_head = lax.dot_general(c_ref[...], head * bf16(-2), NT, preferred_element_type=f32)
        dot_resid = lax.dot_general(c_ref[...], resid, NT, preferred_element_type=f32)
        square = square_ref[...]
        square = jnp.concatenate([square, square], axis=1)
        along = cross - dot_resid
        score = (dot_head + square) + along * along
        score = jnp.where(number == prim, masked_score, score)
        low = jnp.min(score.reshape(LISTS // 8, 8, ROWS), axis=0)
        low = jnp.min(low, axis=0, keepdims=True)
        for k in range(2):
            out_ref[pl.ds(spot, 1), k : k + 1, :] = low[:, k * HALF : (k + 1) * HALF][None]


def scores(name, ids, prefixes, arrays, steps, *last):
    out = jax.ShapeDtypeStruct((N_LIST, 8, HALF), f32)
    return call(
        functools.partial(score_kernel, steps, len(arrays), len(last)),
        name,
        28,
        out if len(last) == 2 else (out, jax.ShapeDtypeStruct((LISTS, 128), f32)),
        ids,
        prefixes,
        *arrays,
        *last,
    )


STEPS = (1, 3, 2)


def move(x, distance, second):
    pairs = []
    for dp in range(N_DP):
        for at in range(N_LIST):
            y, z = divmod(at, SIDE)
            if (dp % 2 == 1) != second:
                y = (y + distance) % SIDE
            else:
                z = (z + distance) % SIDE
            pairs.append((dp * N_LIST + at, dp * N_LIST + y * SIDE + z))
    return lax.ppermute(x, ("dp", "list"), pairs)


def from_other_core(x):
    return lax.ppermute(x, "dp", [(at, at ^ 1) for at in range(N_DP)])


def together(*xs):
    return lax.optimization_barrier(xs)


def local(vectors, centroids, projection, list_ids):
    ids = list_ids.T
    id_rows = ids.reshape(2, N_DP * N_LIST, ROWS)

    prefixes = centroids[:, :PREFIX]
    slots, projection = together(pack(ids, prefixes), projection)
    got = lax.all_to_all(slots, "list", 0, 0, tiled=True)
    rows_out, parts = prepare(ids, centroids, vectors, projection)
    got, rows_out = together(got, rows_out)
    keep, send, head_square = residuals(ids, got, vectors)

    block = jnp.concatenate([keep, from_other_core(send)], axis=0)
    block, rows_out = together(block, rows_out)
    blocks = [block] + [move(block, d, False) for d in STEPS]
    rows_in = lax.all_to_all(rows_out, ("dp", "list"), 0, 0, tiled=True)
    pairs = [jnp.concatenate(blocks[k : k + 2], axis=0) for k in (0, 2)]
    ahead, behind, ahead_too, behind_too = (
        move(pairs[k], STEPS[n], True) for k, n in ((0, 0), (1, 1), (1, 0), (0, 1))
    )
    steps = [[(a, d) for a in (0,) + STEPS] for d in (0,) + STEPS]
    lowest, _ = scores("scores_near", ids, prefixes, blocks, steps[0])
    _, to_far, from_far, rows_in = together(lowest, ahead, behind, rows_in)
    far = [move(to_far, STEPS[0], True), move(from_far, STEPS[1], True)]
    lowest, square = scores("scores_right", ids, prefixes, [ahead, ahead_too], steps[1], lowest)
    lowest = scores("scores_left", ids, prefixes, [behind_too, behind], steps[2], lowest, square)
    lowest = scores("scores_far", ids, prefixes, far, steps[3], lowest, square)
    back = lax.all_to_all(lowest, "list", 0, 0, tiled=True)
    placed = placement(id_rows, rows_in, parts)
    back, placed = together(back, placed)
    low = jnp.min(back[:, :2], axis=0)
    other = from_other_core(low[1:])
    core = lax.axis_index("dp") % 2
    low = jnp.where(iota((2, HALF), 0) == core, low[:1], other)
    lowest_score = (low.reshape(ROWS) + head_square.reshape(ROWS)) / PREFIX
    return placed, lowest_score


def solution(mesh):
    return jax.shard_map(
        local,
        mesh=mesh,
        in_specs=(P(("dp", "list"), None), P("list", None), P(), P()),
        out_specs=(P(("dp", "list"), None), P(("dp", "list"))),
        check_vma=False,
    )
```

```python
import functools

import jax
import jax.numpy as jnp
from jax import lax
from jax.experimental import pallas as pl
from jax.experimental.pallas import tpu as pltpu
from jax.sharding import PartitionSpec as P

PREFIX = 256
N_DP = 8
N_LIST = 16
SIDE = 4
ROWS = 256
HALF = 128
LISTS = 4096
CAP = 8
SLOTS = N_DP * CAP
PDIM = 128

soar_weight = 1.5
masked_score = 1e30
NT = (((1,), (1,)), ((), ()))
bf16 = jnp.bfloat16
f32 = jnp.float32
i32 = jnp.int32


def iota(shape, dim):
    return lax.broadcasted_iota(i32, shape, dim)


def ones_where(mask):
    return jnp.where(mask, 1.0, 0.0)


def dot(a, b):
    return jnp.dot(a, b, preferred_element_type=f32)


def params(mib):
    return pltpu.CompilerParams(vmem_limit_bytes=mib << 20)


def split3(x):
    hi = x.astype(bf16)
    rest = x - hi.astype(f32)
    mid = rest.astype(bf16)
    low = (rest - mid.astype(f32)).astype(bf16)
    return hi, mid, low


def to_column(row, n):
    eye = iota((n, n), 0) == iota((n, n), 1)
    return jnp.sum(jnp.where(eye, jnp.broadcast_to(row, (n, n)), 0.0), axis=1, keepdims=True)


def to_row(column, n):
    eye = iota((n, n), 0) == iota((n, n), 1)
    return jnp.sum(jnp.where(eye, jnp.broadcast_to(column, (n, n)), 0.0), axis=0, keepdims=True)


VMEM = pl.BlockSpec(memory_space=pltpu.VMEM)
HBM = pl.BlockSpec(memory_space=pltpu.HBM)


def places():
    return lax.axis_index("dp"), lax.axis_index("list")


def call(kernel, name, mib, out_shape, *operands, hbm=(), scratch=()):
    return pl.pallas_call(
        kernel,
        out_shape=out_shape,
        in_specs=[HBM if n in hbm else VMEM for n in range(len(operands))],
        out_specs=jax.tree.map(lambda _: VMEM, out_shape),
        scratch_shapes=scratch,
        compiler_params=params(mib),
        name=name,
    )(*operands)


def pack_kernel(ids_ref, c_ref, out_ref):
    group, list_place = places()
    upto = ones_where(iota((ROWS, ROWS), 0) <= iota((ROWS, ROWS), 1)).astype(bf16)
    base = group * (N_LIST * ROWS)
    ids = jnp.concatenate(
        [
            ids_ref[0:1, pl.ds(pl.multiple_of(base + s * ROWS, ROWS), ROWS)]
            for s in range(N_LIST)
        ],
        axis=0,
    )
    inside = (ids >> 12) == list_place
    count = dot(ones_where(inside).astype(bf16), upto)
    rank = jnp.where(inside, count - 1.0, -1.0)
    local = (ids & (LISTS - 1)).astype(f32) + 1.0
    slot = iota((SLOTS, ROWS), 0).astype(f32)
    lane = iota((4 * SLOTS, LISTS), 1).astype(f32)
    for g in range(N_LIST // 4):
        picks = []
        for s in range(4 * g, 4 * g + 4):
            hit = slot == rank[s : s + 1, :]
            picks.append(jnp.sum(jnp.where(hit, local[s : s + 1, :], 0.0), axis=1, keepdims=True))
        pick = jnp.concatenate(picks, axis=0) - 1.0
        hot = ones_where(lane == pick).astype(bf16)
        out_ref[4 * g : 4 * g + 4] = (
            dot(hot, c_ref[...]).astype(bf16).reshape(4, SLOTS, PREFIX)
        )


def pack(ids, prefixes):
    shape = jax.ShapeDtypeStruct((N_LIST, SLOTS, PREFIX), bf16)
    return call(pack_kernel, "pack_prefixes", 16, shape, ids, prefixes)


def residual_kernel(
    ids_ref, got_ref, vec_hbm, keep_ref, send_ref, square_ref, head_ref, resid_ref, sem
):
    group, own = places()
    fetch = pltpu.make_async_copy(vec_hbm.at[:, pl.ds(0, PREFIX)], head_ref, sem)
    fetch.start()
    at = pl.multiple_of((group * N_LIST + own) * ROWS, ROWS)
    shard = ids_ref[0:1, pl.ds(at, ROWS)] >> 12
    member = iota((N_LIST, ROWS), 0) == shard
    upto = ones_where(iota((ROWS, ROWS), 0) <= iota((ROWS, ROWS), 1)).astype(bf16)
    count = dot(ones_where(member).astype(bf16), upto)
    rank = jnp.sum(jnp.where(member, count - 1.0, 0.0), axis=0, keepdims=True)
    slot = to_column((shard * SLOTS).astype(f32) + rank, ROWS)
    hot = ones_where(iota((ROWS, N_LIST * SLOTS), 1).astype(f32) == slot).astype(bf16)
    primary = dot(hot, got_ref[...].reshape(N_LIST * SLOTS, PREFIX))
    fetch.wait()
    head = head_ref[...].astype(f32)
    resid = (head - primary).astype(bf16).astype(f32)
    power = jnp.sum(resid * resid, axis=1, keepdims=True) * (1.0 / PREFIX) + 1e-6
    scale = jnp.sqrt(soar_weight / (PREFIX * power))
    resid_ref[...] = (resid * scale).astype(bf16)
    square_ref[...] = to_row(jnp.sum(head * head, axis=1, keepdims=True), ROWS)
    core = group % 2
    for half, to in ((core, keep_ref), (1 - core, send_ref)):
        rows = pl.ds(pl.multiple_of(half * HALF, HALF), HALF)
        to[:HALF] = head_ref[rows, :]
        to[HALF:] = resid_ref[rows, :]


def residuals(ids, got, vectors):
    halves = jax.ShapeDtypeStruct((2 * HALF, PREFIX), bf16)
    shape = (halves, halves, jax.ShapeDtypeStruct((1, ROWS), f32))
    scratch = [pltpu.VMEM((ROWS, PREFIX), bf16)] * 2 + [pltpu.SemaphoreType.DMA]
    return call(
        residual_kernel, "own_residuals", 8, shape, ids, got, vectors, hbm=(2,), scratch=scratch
    )


def rank_tables(first, second):
    before = ones_where(iota((ROWS, ROWS), 0) < iota((ROWS, ROWS), 1)).astype(bf16)
    one0, one1 = ones_where(first), ones_where(second)
    earlier = dot((one0 + one1).astype(bf16), before)
    return jnp.where(first, earlier, -1.0), jnp.where(second, earlier + one0, -1.0)


def eightfold(table):
    n = table.shape[0]
    return jnp.broadcast_to(table[:, None, :], (n, CAP, ROWS)).reshape(n * CAP, ROWS)


def prepare_kernel(
    ids_ref, c_hbm, vec_hbm, proj_ref, rows_ref, parts_ref, c_ref, vec_ref, sems
):
    group, own = places()
    step_rows = LISTS // 8
    wide = pltpu.make_async_copy(vec_hbm, vec_ref, sems.at[8])
    wide.start()
    copies = [
        pltpu.make_async_copy(
            c_hbm.at[pl.ds(n * step_rows, step_rows)],
            c_ref.at[pl.ds(n * step_rows, step_rows)],
            sems.at[n],
        )
        for n in range(8)
    ]
    for copy in copies:
        copy.start()
    at = pl.multiple_of((group * N_LIST + own) * ROWS, ROWS)
    devices = N_DP * N_LIST
    hits = []
    for k in range(2):
        ids = ids_ref[k : k + 1, pl.ds(at, ROWS)]
        hits.append(iota((devices, ROWS), 0) == (ids & (N_DP - 1)) * N_LIST + (ids >> 12))
    rank0, rank1 = rank_tables(*hits)
    slot = (iota((devices * CAP, ROWS), 0) & (CAP - 1)).astype(f32)
    hot = ones_where((eightfold(rank0) == slot) | (eightfold(rank1) == slot)).astype(bf16)
    wide.wait()
    payload = dot(vec_ref[...], proj_ref[...]).astype(bf16)
    rows_ref[...] = dot(hot, payload).astype(bf16).reshape(devices, CAP, PDIM)
    per = step_rows // N_DP
    chosen = iota((per, step_rows), 1) == N_DP * iota((per, step_rows), 0) + group
    chosen = ones_where(chosen).astype(bf16)
    for n, copy in enumerate(copies):
        copy.wait()
        mine = dot(chosen, c_ref[n * step_rows : (n + 1) * step_rows]).astype(bf16)
        for k, part in enumerate(split3(dot(mine, proj_ref[...]))):
            parts_ref[k, n * per : (n + 1) * per] = part


def prepare(ids, centroids, vectors, projection):
    shape = (
        jax.ShapeDtypeStruct((N_DP * N_LIST, CAP, PDIM), bf16),
        jax.ShapeDtypeStruct((3, LISTS // N_DP, PDIM), bf16),
    )
    scratch = [
        pltpu.VMEM(centroids.shape, bf16),
        pltpu.VMEM(vectors.shape, bf16),
        pltpu.SemaphoreType.DMA((9,)),
    ]
    return call(
        prepare_kernel, "prepare_rows", 56, shape, ids, centroids, vectors, projection, hbm=(1, 2), scratch=scratch
    )


def place_kernel(ids_ref, got_ref, parts_ref, out_ref):
    group, own = places()
    devices = N_DP * N_LIST
    hits, local = [], []
    for k in range(2):
        ids = ids_ref[k]
        hits.append(((ids & (N_DP - 1)) == group) & ((ids >> 12) == own))
        local.append(((ids & (LISTS - 1)) >> 3).astype(f32) + 1.0)
    rank0, rank1 = rank_tables(*hits)
    slot = (iota((devices * CAP, ROWS), 0) & (CAP - 1)).astype(f32)
    pick = jnp.where(eightfold(rank0) == slot, eightfold(local[0]), 0.0)
    pick += jnp.where(eightfold(rank1) == slot, eightfold(local[1]), 0.0)
    pick = jnp.sum(pick, axis=1, keepdims=True) - 1.0
    per_owner = LISTS // N_DP
    hot = ones_where(iota((devices * CAP, per_owner), 1).astype(f32) == pick).astype(bf16)
    centroid = dot(hot, parts_ref[0]) + dot(hot, parts_ref[1]) + dot(hot, parts_ref[2])
    got = got_ref[...].reshape(devices * CAP, PDIM).astype(f32)
    out_ref[...] = jnp.where(pick >= 0.0, got - centroid, 0.0).astype(bf16)


def placement(ids, got, parts):
    shape = jax.ShapeDtypeStruct((N_DP * N_LIST * CAP, PDIM), bf16)
    return call(place_kernel, "place_rows", 12, shape, ids, got, parts)


def squares_of(rows):
    square = jnp.square(rows.astype(f32))
    upper = square.astype(bf16)
    lower = (square - upper.astype(f32)).astype(bf16)
    one = jnp.ones((PREFIX, 128), bf16)
    return dot(upper, one) + dot(lower, one)


def score_kernel(steps, n_arrays, given, *refs):
    ids_ref, c_ref = refs[:2]
    arrays = refs[2 : 2 + n_arrays]
    rest = refs[2 + n_arrays :]
    if given == 2:
        square_ref, out_ref = rest[1:]
    else:
        out_ref, square_ref = rest[given:]
        square_ref[...] = squares_of(c_ref[...])
    out_ref[...] = rest[0][...] if given else jnp.zeros(out_ref.shape, f32)
    group, own = places()
    core = group % 2
    eye = iota((ROWS, ROWS), 0) == iota((ROWS, ROWS), 1)
    number = iota((LISTS, ROWS), 0)
    for n, (one, two) in enumerate(steps):
        dy = two + core * (one - two)
        dz = one + core * (two - one)
        spot = (own // SIDE + SIDE - dy) % SIDE * SIDE + (own % SIDE + SIDE - dz) % SIDE
        prims = []
        for k in range(2):
            device = (group + k * (1 - 2 * core)) * N_LIST + spot
            lane = pl.multiple_of(device * ROWS + core * HALF, HALF)
            prims.append(ids_ref[0:1, pl.ds(lane, HALF)] - own * LISTS)
        prim = jnp.concatenate(prims, axis=1)
        each = len(steps) // n_arrays
        ref, at = arrays[n // each], n % each * 2 * ROWS
        parts = [ref[at + k * HALF : at + (k + 1) * HALF] for k in range(4)]
        head = jnp.concatenate([parts[0], parts[2]], axis=0)
        resid = jnp.concatenate([parts[1], parts[3]], axis=0)
        both = lax.dot_general(head, resid, NT, preferred_element_type=f32)
        cross = jnp.sum(jnp.where(eye, both, 0.0), axis=0, keepdims=True)
        dot_head = lax.dot_general(c_ref[...], head * bf16(-2), NT, preferred_element_type=f32)
        dot_resid = lax.dot_general(c_ref[...], resid, NT, preferred_element_type=f32)
        square = square_ref[...]
        square = jnp.concatenate([square, square], axis=1)
        along = cross - dot_resid
        score = (dot_head + square) + along * along
        score = jnp.where(number == prim, masked_score, score)
        low = jnp.min(score.reshape(LISTS // 8, 8, ROWS), axis=0)
        low = jnp.min(low, axis=0, keepdims=True)
        for k in range(2):
            out_ref[pl.ds(spot, 1), k : k + 1, :] = low[:, k * HALF : (k + 1) * HALF][None]


def scores(name, ids, prefixes, arrays, steps, *last):
    out = jax.ShapeDtypeStruct((N_LIST, 8, HALF), f32)
    return call(
        functools.partial(score_kernel, steps, len(arrays), len(last)),
        name,
        28,
        (out, jax.ShapeDtypeStruct((LISTS, 128), f32)) if len(last) == 1 else out,
        ids,
        prefixes,
        *arrays,
        *last,
        scratch=[] if last else [pltpu.VMEM((LISTS, 128), f32)],
    )


STEPS = (1, 3, 2)


def move(x, distance, second):
    pairs = []
    for dp in range(N_DP):
        for at in range(N_LIST):
            y, z = divmod(at, SIDE)
            if (dp % 2 == 1) != second:
                y = (y + distance) % SIDE
            else:
                z = (z + distance) % SIDE
            pairs.append((dp * N_LIST + at, dp * N_LIST + y * SIDE + z))
    return lax.ppermute(x, ("dp", "list"), pairs)


def from_other_core(x):
    return lax.ppermute(x, "dp", [(at, at ^ 1) for at in range(N_DP)])


def together(*xs):
    return lax.optimization_barrier(xs)


def local(vectors, centroids, projection, list_ids):
    ids = list_ids.T
    id_rows = ids.reshape(2, N_DP * N_LIST, ROWS)

    prefixes = centroids[:, :PREFIX]
    slots, projection = together(pack(ids, prefixes), projection)
    got = lax.all_to_all(slots, "list", 0, 0, tiled=True)
    rows_out, parts = prepare(ids, centroids, vectors, projection)
    got, rows_out = together(got, rows_out)
    keep, send, head_square = residuals(ids, got, vectors)

    block = jnp.concatenate([keep, from_other_core(send)], axis=0)
    block, rows_out = together(block, rows_out)
    blocks = [block] + [move(block, d, False) for d in STEPS]
    rows_in = lax.all_to_all(rows_out, ("dp", "list"), 0, 0, tiled=True)
    pairs = [jnp.concatenate(blocks[k : k + 2], axis=0) for k in (0, 2)]
    ahead, behind, ahead_too, behind_too = (
        move(pairs[k], STEPS[n], True) for k, n in ((0, 0), (1, 1), (1, 0), (0, 1))
    )
    steps = [[(a, d) for a in (0,) + STEPS] for d in (0,) + STEPS]
    lowest = scores("scores_near", ids, prefixes, blocks, steps[0])
    _, to_far, from_far, rows_in = together(lowest, ahead, behind, rows_in)
    far = [move(to_far, STEPS[0], True), move(from_far, STEPS[1], True)]
    sides = [ahead, ahead_too, behind_too, behind]
    lowest, square = scores("scores_sides", ids, prefixes, sides, steps[1] + steps[2], lowest)
    lowest = scores("scores_far", ids, prefixes, far, steps[3], lowest, square)
    back = lax.all_to_all(lowest, "list", 0, 0, tiled=True)
    placed = placement(id_rows, rows_in, parts)
    back, placed = together(back, placed)
    low = jnp.min(back[:, :2], axis=0)
    other = from_other_core(low[1:])
    core = lax.axis_index("dp") % 2
    low = jnp.where(iota((2, HALF), 0) == core, low[:1], other)
    lowest_score = (low.reshape(ROWS) + head_square.reshape(ROWS)) / PREFIX
    return placed, lowest_score


def solution(mesh):
    return jax.shard_map(
        local,
        mesh=mesh,
        in_specs=(P(("dp", "list"), None), P("list", None), P(), P()),
        out_specs=(P(("dp", "list"), None), P(("dp", "list"))),
        check_vma=False,
    )
```

```python
import functools

import jax
import jax.numpy as jnp
from jax import lax
from jax.experimental import pallas as pl
from jax.experimental.pallas import tpu as pltpu
from jax.sharding import PartitionSpec as P

PREFIX = 256
N_DP = 8
N_LIST = 16
SIDE = 4
ROWS = 256
HALF = 128
LISTS = 4096
CAP = 8
SLOTS = N_DP * CAP
PDIM = 128

soar_weight = 1.5
masked_score = 1e30
NT = (((1,), (1,)), ((), ()))
bf16 = jnp.bfloat16
f32 = jnp.float32
i32 = jnp.int32


def iota(shape, dim):
    return lax.broadcasted_iota(i32, shape, dim)


def ones_where(mask):
    return jnp.where(mask, 1.0, 0.0)


def dot(a, b):
    return jnp.dot(a, b, preferred_element_type=f32)


def params(mib):
    return pltpu.CompilerParams(vmem_limit_bytes=mib << 20)


def split3(x):
    hi = x.astype(bf16)
    rest = x - hi.astype(f32)
    mid = rest.astype(bf16)
    low = (rest - mid.astype(f32)).astype(bf16)
    return hi, mid, low


def to_column(row, n):
    eye = iota((n, n), 0) == iota((n, n), 1)
    return jnp.sum(jnp.where(eye, jnp.broadcast_to(row, (n, n)), 0.0), axis=1, keepdims=True)


def to_row(column, n):
    eye = iota((n, n), 0) == iota((n, n), 1)
    return jnp.sum(jnp.where(eye, jnp.broadcast_to(column, (n, n)), 0.0), axis=0, keepdims=True)


VMEM = pl.BlockSpec(memory_space=pltpu.VMEM)
HBM = pl.BlockSpec(memory_space=pltpu.HBM)


def places():
    return lax.axis_index("dp"), lax.axis_index("list")


def call(kernel, name, mib, out_shape, *operands, hbm=(), scratch=()):
    return pl.pallas_call(
        kernel,
        out_shape=out_shape,
        in_specs=[HBM if n in hbm else VMEM for n in range(len(operands))],
        out_specs=jax.tree.map(lambda _: VMEM, out_shape),
        scratch_shapes=scratch,
        compiler_params=params(mib),
        name=name,
    )(*operands)


def pack_kernel(ids_ref, c_ref, out_ref):
    group, list_place = places()
    upto = ones_where(iota((ROWS, ROWS), 0) <= iota((ROWS, ROWS), 1)).astype(bf16)
    base = group * (N_LIST * ROWS)
    ids = jnp.concatenate(
        [
            ids_ref[0:1, pl.ds(pl.multiple_of(base + s * ROWS, ROWS), ROWS)]
            for s in range(N_LIST)
        ],
        axis=0,
    )
    inside = (ids >> 12) == list_place
    count = dot(ones_where(inside).astype(bf16), upto)
    rank = jnp.where(inside, count - 1.0, -1.0)
    local = (ids & (LISTS - 1)).astype(f32) + 1.0
    slot = iota((SLOTS, ROWS), 0).astype(f32)
    lane = iota((4 * SLOTS, LISTS), 1).astype(f32)
    for g in range(N_LIST // 4):
        picks = []
        for s in range(4 * g, 4 * g + 4):
            hit = slot == rank[s : s + 1, :]
            picks.append(jnp.sum(jnp.where(hit, local[s : s + 1, :], 0.0), axis=1, keepdims=True))
        pick = jnp.concatenate(picks, axis=0) - 1.0
        hot = ones_where(lane == pick).astype(bf16)
        out_ref[4 * g : 4 * g + 4] = (
            dot(hot, c_ref[...]).astype(bf16).reshape(4, SLOTS, PREFIX)
        )


def pack(ids, prefixes):
    shape = jax.ShapeDtypeStruct((N_LIST, SLOTS, PREFIX), bf16)
    return call(pack_kernel, "pack_prefixes", 16, shape, ids, prefixes)


def residual_kernel(
    ids_ref, got_ref, vec_hbm, keep_ref, send_ref, square_ref, head_ref, resid_ref, sem
):
    group, own = places()
    fetch = pltpu.make_async_copy(vec_hbm.at[:, pl.ds(0, PREFIX)], head_ref, sem)
    fetch.start()
    at = pl.multiple_of((group * N_LIST + own) * ROWS, ROWS)
    shard = ids_ref[0:1, pl.ds(at, ROWS)] >> 12
    member = iota((N_LIST, ROWS), 0) == shard
    upto = ones_where(iota((ROWS, ROWS), 0) <= iota((ROWS, ROWS), 1)).astype(bf16)
    count = dot(ones_where(member).astype(bf16), upto)
    rank = jnp.sum(jnp.where(member, count - 1.0, 0.0), axis=0, keepdims=True)
    slot = to_column((shard * SLOTS).astype(f32) + rank, ROWS)
    hot = ones_where(iota((ROWS, N_LIST * SLOTS), 1).astype(f32) == slot).astype(bf16)
    primary = dot(hot, got_ref[...].reshape(N_LIST * SLOTS, PREFIX))
    fetch.wait()
    head = head_ref[...].astype(f32)
    resid = (head - primary).astype(bf16).astype(f32)
    power = jnp.sum(resid * resid, axis=1, keepdims=True) * (1.0 / PREFIX) + 1e-6
    scale = jnp.sqrt(soar_weight / (PREFIX * power))
    resid_ref[...] = (resid * scale).astype(bf16)
    square_ref[...] = to_row(jnp.sum(head * head, axis=1, keepdims=True), ROWS)
    core = group % 2
    for half, to in ((core, keep_ref), (1 - core, send_ref)):
        rows = pl.ds(pl.multiple_of(half * HALF, HALF), HALF)
        to[:HALF] = head_ref[rows, :]
        to[HALF:] = resid_ref[rows, :]


def residuals(ids, got, vectors):
    halves = jax.ShapeDtypeStruct((2 * HALF, PREFIX), bf16)
    shape = (halves, halves, jax.ShapeDtypeStruct((1, ROWS), f32))
    scratch = [pltpu.VMEM((ROWS, PREFIX), bf16)] * 2 + [pltpu.SemaphoreType.DMA]
    return call(
        residual_kernel, "own_residuals", 8, shape, ids, got, vectors, hbm=(2,), scratch=scratch
    )


def rank_tables(first, second):
    before = ones_where(iota((ROWS, ROWS), 0) < iota((ROWS, ROWS), 1)).astype(bf16)
    one0, one1 = ones_where(first), ones_where(second)
    earlier = dot((one0 + one1).astype(bf16), before)
    return jnp.where(first, earlier, -1.0), jnp.where(second, earlier + one0, -1.0)


def eightfold(table):
    n = table.shape[0]
    return jnp.broadcast_to(table[:, None, :], (n, CAP, ROWS)).reshape(n * CAP, ROWS)


def prepare_kernel(
    ids_ref, c_hbm, vec_hbm, proj_ref, rows_ref, parts_ref, c_ref, vec_ref, sems
):
    group, own = places()
    step_rows = LISTS // 8
    wide = pltpu.make_async_copy(vec_hbm, vec_ref, sems.at[8])
    wide.start()
    copies = [
        pltpu.make_async_copy(
            c_hbm.at[pl.ds(n * step_rows, step_rows)],
            c_ref.at[pl.ds(n * step_rows, step_rows)],
            sems.at[n],
        )
        for n in range(8)
    ]
    for copy in copies:
        copy.start()
    at = pl.multiple_of((group * N_LIST + own) * ROWS, ROWS)
    devices = N_DP * N_LIST
    hits = []
    for k in range(2):
        ids = ids_ref[k : k + 1, pl.ds(at, ROWS)]
        hits.append(iota((devices, ROWS), 0) == (ids & (N_DP - 1)) * N_LIST + (ids >> 12))
    rank0, rank1 = rank_tables(*hits)
    slot = (iota((devices * CAP, ROWS), 0) & (CAP - 1)).astype(f32)
    hot = ones_where((eightfold(rank0) == slot) | (eightfold(rank1) == slot)).astype(bf16)
    wide.wait()
    payload = dot(vec_ref[...], proj_ref[...]).astype(bf16)
    rows_ref[...] = dot(hot, payload).astype(bf16).reshape(devices, CAP, PDIM)
    per = step_rows // N_DP
    chosen = iota((per, step_rows), 1) == N_DP * iota((per, step_rows), 0) + group
    chosen = ones_where(chosen).astype(bf16)
    for n, copy in enumerate(copies):
        copy.wait()
        mine = dot(chosen, c_ref[n * step_rows : (n + 1) * step_rows]).astype(bf16)
        for k, part in enumerate(split3(dot(mine, proj_ref[...]))):
            parts_ref[k, n * per : (n + 1) * per] = part


def prepare(ids, centroids, vectors, projection):
    shape = (
        jax.ShapeDtypeStruct((N_DP * N_LIST, CAP, PDIM), bf16),
        jax.ShapeDtypeStruct((3, LISTS // N_DP, PDIM), bf16),
    )
    scratch = [
        pltpu.VMEM(centroids.shape, bf16),
        pltpu.VMEM(vectors.shape, bf16),
        pltpu.SemaphoreType.DMA((9,)),
    ]
    return call(
        prepare_kernel, "prepare_rows", 56, shape, ids, centroids, vectors, projection, hbm=(1, 2), scratch=scratch
    )


def place_kernel(ids_ref, got_ref, parts_ref, out_ref):
    group, own = places()
    devices = N_DP * N_LIST
    hits, local = [], []
    for k in range(2):
        ids = ids_ref[k]
        hits.append(((ids & (N_DP - 1)) == group) & ((ids >> 12) == own))
        local.append(((ids & (LISTS - 1)) >> 3).astype(f32) + 1.0)
    rank0, rank1 = rank_tables(*hits)
    slot = (iota((devices * CAP, ROWS), 0) & (CAP - 1)).astype(f32)
    pick = jnp.where(eightfold(rank0) == slot, eightfold(local[0]), 0.0)
    pick += jnp.where(eightfold(rank1) == slot, eightfold(local[1]), 0.0)
    pick = jnp.sum(pick, axis=1, keepdims=True) - 1.0
    per_owner = LISTS // N_DP
    hot = ones_where(iota((devices * CAP, per_owner), 1).astype(f32) == pick).astype(bf16)
    centroid = dot(hot, parts_ref[0]) + dot(hot, parts_ref[1]) + dot(hot, parts_ref[2])
    got = got_ref[...].reshape(devices * CAP, PDIM).astype(f32)
    out_ref[...] = jnp.where(pick >= 0.0, got - centroid, 0.0).astype(bf16)


def placement(ids, got, parts):
    shape = jax.ShapeDtypeStruct((N_DP * N_LIST * CAP, PDIM), bf16)
    return call(place_kernel, "place_rows", 12, shape, ids, got, parts)


def squares_of(rows):
    square = jnp.square(rows.astype(f32))
    upper = square.astype(bf16)
    lower = (square - upper.astype(f32)).astype(bf16)
    one = jnp.ones((PREFIX, 128), bf16)
    return dot(upper, one) + dot(lower, one)


def score_kernel(steps, n_arrays, given, *refs):
    ids_ref, c_ref = refs[:2]
    arrays = refs[2 : 2 + n_arrays]
    rest = refs[2 + n_arrays :]
    if given == 2:
        square_ref, out_ref = rest[1:]
    else:
        out_ref, square_ref = rest[given:]
        square_ref[...] = squares_of(c_ref[...])
    out_ref[...] = rest[0][...] if given else jnp.zeros(out_ref.shape, f32)
    group, own = places()
    core = group % 2
    eye = iota((ROWS, ROWS), 0) == iota((ROWS, ROWS), 1)
    number = iota((LISTS, ROWS), 0)
    for n, (one, two) in enumerate(steps):
        dy = two + core * (one - two)
        dz = one + core * (two - one)
        spot = (own // SIDE + SIDE - dy) % SIDE * SIDE + (own % SIDE + SIDE - dz) % SIDE
        prims = []
        for k in range(2):
            device = (group + k * (1 - 2 * core)) * N_LIST + spot
            lane = pl.multiple_of(device * ROWS + core * HALF, HALF)
            prims.append(ids_ref[0:1, pl.ds(lane, HALF)] - own * LISTS)
        prim = jnp.concatenate(prims, axis=1)
        each = len(steps) // n_arrays
        ref, at = arrays[n // each], n % each * 2 * ROWS
        parts = [ref[at + k * HALF : at + (k + 1) * HALF] for k in range(4)]
        head = jnp.concatenate([parts[0], parts[2]], axis=0)
        resid = jnp.concatenate([parts[1], parts[3]], axis=0)
        both = lax.dot_general(head, resid, NT, preferred_element_type=f32)
        cross = jnp.sum(jnp.where(eye, both, 0.0), axis=0, keepdims=True)
        dot_head = lax.dot_general(c_ref[...], head * bf16(-2), NT, preferred_element_type=f32)
        dot_resid = lax.dot_general(c_ref[...], resid, NT, preferred_element_type=f32)
        square = square_ref[...]
        square = jnp.concatenate([square, square], axis=1)
        along = cross - dot_resid
        score = (dot_head + square) + along * along
        score = jnp.where(number == prim, masked_score, score)
        low = jnp.min(score.reshape(LISTS // 8, 8, ROWS), axis=0)
        low = jnp.min(low, axis=0, keepdims=True)
        for k in range(2):
            out_ref[pl.ds(spot, 1), k : k + 1, :] = low[:, k * HALF : (k + 1) * HALF][None]


def scores(name, ids, prefixes, arrays, steps, *last):
    out = jax.ShapeDtypeStruct((N_LIST, 2, HALF), f32)
    return call(
        functools.partial(score_kernel, steps, len(arrays), len(last)),
        name,
        28,
        (out, jax.ShapeDtypeStruct((LISTS, 128), f32)) if len(last) == 1 else out,
        ids,
        prefixes,
        *arrays,
        *last,
        scratch=[] if last else [pltpu.VMEM((LISTS, 128), f32)],
    )


STEPS = (1, 3, 2)


def move(x, distance, second):
    pairs = []
    for dp in range(N_DP):
        for at in range(N_LIST):
            y, z = divmod(at, SIDE)
            if (dp % 2 == 1) != second:
                y = (y + distance) % SIDE
            else:
                z = (z + distance) % SIDE
            pairs.append((dp * N_LIST + at, dp * N_LIST + y * SIDE + z))
    return lax.ppermute(x, ("dp", "list"), pairs)


def from_other_core(x):
    return lax.ppermute(x, "dp", [(at, at ^ 1) for at in range(N_DP)])


def together(*xs):
    return lax.optimization_barrier(xs)


def local(vectors, centroids, projection, list_ids):
    ids = list_ids.T
    id_rows = ids.reshape(2, N_DP * N_LIST, ROWS)

    prefixes = centroids[:, :PREFIX]
    slots, projection = together(pack(ids, prefixes), projection)
    got = lax.all_to_all(slots, "list", 0, 0, tiled=True)
    rows_out, parts = prepare(ids, centroids, vectors, projection)
    got, rows_out = together(got, rows_out)
    keep, send, head_square = residuals(ids, got, vectors)

    block = jnp.concatenate([keep, from_other_core(send)], axis=0)
    block, rows_out = together(block, rows_out)
    blocks = [block] + [move(block, d, False) for d in STEPS]
    rows_in = lax.all_to_all(rows_out, ("dp", "list"), 0, 0, tiled=True)
    pairs = [jnp.concatenate(blocks[k : k + 2], axis=0) for k in (0, 2)]
    ahead, behind_too, behind, ahead_too = (
        move(pairs[k], STEPS[n], True) for k, n in ((0, 0), (0, 1), (1, 1), (1, 0))
    )
    steps = [[(a, d) for a in (0,) + STEPS] for d in (0,) + STEPS]
    lowest = scores("scores_near", ids, prefixes, blocks, steps[0])
    _, to_far, from_far, behind_too, rows_in = together(lowest, ahead, behind, behind_too, rows_in)
    far = [move(to_far, STEPS[0], True), move(from_far, STEPS[1], True)]
    sides = [ahead, ahead_too, behind_too, behind]
    lowest, square = scores("scores_sides", ids, prefixes, sides, steps[1] + steps[2], lowest)
    lowest = scores("scores_far", ids, prefixes, far, steps[3], lowest, square)
    back = lax.all_to_all(lowest, "list", 0, 0, tiled=True)
    placed = placement(id_rows, rows_in, parts)
    back, placed = together(back, placed)
    low = jnp.min(back, axis=0)
    other = from_other_core(low[1:])
    core = lax.axis_index("dp") % 2
    low = jnp.where(iota((2, HALF), 0) == core, low[:1], other)
    lowest_score = (low.reshape(ROWS) + head_square.reshape(ROWS)) / PREFIX
    return placed, lowest_score


def solution(mesh):
    return jax.shard_map(
        local,
        mesh=mesh,
        in_specs=(P(("dp", "list"), None), P("list", None), P(), P()),
        out_specs=(P(("dp", "list"), None), P(("dp", "list"))),
        check_vma=False,
    )
```
